32 devices in a mesh: row: 8 (over y, x, core), col: 4 (over z).
Axes of the slice: x: 2, y: 2, z: 4, core: 2. Of those that a mesh axis runs over, the one named last changes fastest.
Arguments:
- vectors: float32 [96, 65536], P(None, ('col', 'row')), may hold values from -6 to 6
- blocks: float32 [8, 4, 176, 128, 128], P('row', 'col'), may hold values from -0.15625 to 0.15625
- block_row: int32 [8, 4, 176], P('row', 'col'), may hold values from 0 to 63
- block_col: int32 [8, 4, 176], P('row', 'col'), may hold values from 0 to 127
- block_count: int32 [8, 4], P('row', 'col'), may hold values from 22 to 176, as said below
- lower_bound: float32 [1], replicated, may hold values from -2.5 to -1.5
- upper_bound: float32 [1], replicated, may hold values from 1.5 to 2.5
Outputs:
- filtered: float32 [96, 65536], P(None, ('col', 'row'))
The draws below stay inside these ranges and needn't reach their ends.
Inputs may be any that keep to these rules, and one draw needn't show every extreme that they name: `block_row`: local block row index within the device's band. `block_col`: local block column index within the device's band. `block_count`: in every row of the device grid one device has all 176 slots stored.
All inputs are finite; a program needn't handle non-finite values.
Results may differ from the reference program's by a relative error of at most 0.0003.
Values sent between devices are 32-bit elements; how exact they have to be, the bound alone decides.
A program may use at most 128 MiB of HBM per device.

```python
import jax
import jax.numpy as jnp
from jax import lax

N = 65536
BS = 128
VECS = 96
MAXB = 176
DEGREE = 2
RB = 64
CB = 128
N_ROW = 8
N_COL = 4


def draw_block_count(key, part):
    first_key, second_key = jax.random.split(jax.random.fold_in(key, 17))
    base_count = jax.random.randint(first_key, (N_ROW, N_COL), MAXB // 8, MAXB // 2 + 1)
    full_column = jax.random.randint(second_key, (N_ROW,), 0, N_COL)
    hit_mask = jnp.arange(N_COL)[None, :] == full_column[:, None]
    return jnp.where(hit_mask, MAXB, base_count).astype(jnp.int32)


def set_ends(values, stream_key, least, high):
    index_at = [jax.random.randint(jax.random.fold_in(stream_key, axis), (), 0, length) for axis, length in enumerate(values.shape)]
    main_axis = values.shape.index(max(values.shape))
    neighbour = index_at[:main_axis] + [(index_at[main_axis] + 1) % values.shape[main_axis]] + index_at[main_axis + 1:]
    return values.at[tuple(index_at)].set(least).at[tuple(neighbour)].set(high)


def levels(own_key, shape, shards, low, high):
    def one(axis_at, parts):
        draws = jax.random.uniform(jax.random.fold_in(jax.random.fold_in(own_key, 6), axis_at), (parts,), jnp.float32, low / len(shards), high / len(shards))
        return jnp.repeat(jnp.exp(draws), shape[axis_at] // parts).reshape((-1,) + (1,) * (len(shape) - axis_at - 1))

    factor_of = one(*shards[0])
    for cut in shards[1:]:
        factor_of = factor_of * one(*cut)
    return factor_of


def gaussian(own_key, extent, deviation, most, cuts=(), held_as=jnp.bfloat16):
    values = jax.random.normal(own_key, extent, jnp.float32) * deviation
    if len(cuts) > 0:
        values = levels(own_key, extent, cuts, -0.22, 0.18) * values
    return jnp.clip(values, min=-most, max=most).astype(held_as)


def setup_inputs(seed: int = 0) -> dict:
    streams_of = jax.random.split(jax.random.key(seed), 8)
    return {
        "vectors": gaussian(streams_of[0], (VECS, N), 1.0, 6.0, ((1, 32),), jnp.float32),
        "blocks": gaussian(streams_of[1], (N_ROW, N_COL, MAXB, BS, BS), (MAXB * N_ROW * N_COL * BS * BS // N) ** -0.5, 0.15625, ((0, 8), (1, 4)), jnp.float32),
        "block_row": set_ends(jax.random.randint(streams_of[2], (N_ROW, N_COL, MAXB), 0, RB), jax.random.fold_in(streams_of[2], 1), 0, RB - 1).astype(jnp.int32),
        "block_col": set_ends(jax.random.randint(streams_of[3], (N_ROW, N_COL, MAXB), 0, CB), jax.random.fold_in(streams_of[3], 1), 0, CB - 1).astype(jnp.int32),
        "block_count": draw_block_count(jax.random.fold_in(streams_of[7], 71), 0),
        "lower_bound": jnp.clip(jax.random.uniform(streams_of[5], (1,), jnp.float32, -2.5, -1.5), -2.5, -1.5),
        "upper_bound": jnp.clip(jax.random.uniform(streams_of[6], (1,), jnp.float32, 1.5, 2.5), 1.5, 2.5),
    }


def hamiltonian_product(vectors, blocks, block_row, block_col, block_count):
    block_total = N // BS
    vec_blocks = vectors.reshape(VECS, block_total, BS)
    flat_blocks = blocks.reshape(N_ROW * N_COL, MAXB, BS, BS)
    flat_rows = block_row.reshape(N_ROW * N_COL, MAXB)
    flat_cols = block_col.reshape(N_ROW * N_COL, MAXB)
    flat_count = block_count.reshape(N_ROW * N_COL)
    device_ids = jnp.arange(N_ROW * N_COL, dtype=jnp.int32)

    def visit_device(accumulated, inputs):
        device_blocks, rows_local, cols_local, slot_count, device_id = inputs
        global_row = (device_id // N_COL) * RB + rows_local
        global_col = (device_id % N_COL) * CB + cols_local
        live_mask = (jnp.arange(MAXB) < slot_count).astype(jnp.float32)
        source_col = jnp.take(vec_blocks, global_col, axis=1)
        forward = jnp.einsum("sij,vsj->vsi", device_blocks, source_col, precision=lax.Precision.HIGHEST)
        forward = forward * live_mask[None, :, None]
        source_row = jnp.take(vec_blocks, global_row, axis=1)
        backward = jnp.einsum("sij,vsi->vsj", device_blocks, source_row, precision=lax.Precision.HIGHEST)
        backward = backward * live_mask[None, :, None]
        accumulated = accumulated.at[:, global_row].add(forward)
        accumulated = accumulated.at[:, global_col].add(backward)
        return accumulated, None

    start = jnp.zeros((VECS, block_total, BS), jnp.float32)
    result, _ = lax.scan(visit_device, start, (flat_blocks, flat_rows, flat_cols, flat_count, device_ids))
    return result.reshape(VECS, N)


def reference(vectors, blocks, block_row, block_col, block_count, lower_bound, upper_bound):
    center = (upper_bound[0] + lower_bound[0]) / 2.0
    half_width = (upper_bound[0] - lower_bound[0]) / 2.0
    previous = vectors
    current = (hamiltonian_product(vectors, blocks, block_row, block_col, block_count) - center * vectors) / half_width
    for iteration in range(DEGREE - 1):
        product = hamiltonian_product(current, blocks, block_row, block_col, block_count)
        following = 2.0 * (product - center * current) / half_width - previous
        previous, current = current, following
    return current
```

```python
import functools

import jax
import jax.numpy as jnp
from jax import lax
from jax.experimental import pallas as pl
from jax.experimental.pallas import tpu as pltpu
from jax.sharding import PartitionSpec as P

BS = 128
VMEM_BYTES = 56 * 1024 * 1024
MESH = pl.DeviceIdType.MESH


def parts_of(total, most):
    best = 1
    for size in range(1, most + 1):
        if total % size == 0:
            best = size
    return best


def remote(src, dst, send_sem, recv_sem, row, col):
    return pltpu.make_async_remote_copy(
        src_ref=src,
        dst_ref=dst,
        send_sem=send_sem,
        recv_sem=recv_sem,
        device_id=(row, col),
        device_id_type=MESH,
    )


def gather_kernel(rows, chunks, x_ref, out_ref, local_sem, send_sem, recv_sem, fsend_sem, frecv_sem):
    half = rows // 2
    size = x_ref.shape[0]
    step = size // chunks
    r, c = lax.axis_index("row"), lax.axis_index("col")
    q, k = r // 2, r % 2
    sibling = r + 1 - 2 * k
    barrier = pltpu.get_barrier_semaphore()
    for d in range(1, half):
        pl.semaphore_signal(barrier, inc=1, device_id=((q + d) % half * 2 + k, c), device_id_type=MESH)
    pl.semaphore_signal(barrier, inc=1, device_id=(sibling, c), device_id_type=MESH)
    pl.semaphore_wait(barrier, half)

    def slot(owner, j):
        return out_ref.at[pl.ds(owner * size + j * step, step)]

    def send(d, j):
        return remote(x_ref.at[pl.ds(j * step, step)], slot(r, j), send_sem.at[d, j], recv_sem.at[d, j],
                      (q + d) % half * 2 + k, c)

    def pass_on(d, j):
        owner = (q + half - d) % half * 2 + k
        source = x_ref.at[pl.ds(j * step, step)] if d == 0 else slot(owner, j)
        return remote(source, slot(owner, j), fsend_sem.at[d, j], frecv_sem.at[d, j], sibling, c)

    for j in range(chunks):
        for d in range(1, half):
            send(d, j).start()
    for j in range(chunks):
        pass_on(0, j).start()
    own = pltpu.make_async_copy(x_ref, out_ref.at[pl.ds(r * size, size)], local_sem)
    own.start()
    for j in range(chunks):
        for d in range(1, half):
            send(d, j).wait_recv()
            pass_on(d, j).start()
    own.wait()
    for j in range(chunks):
        for d in range(half):
            pass_on(d, j).wait_recv()
            pass_on(d, j).wait_send()
            if d > 0:
                send(d, j).wait_send()


def gather(x, rows):
    size = x.shape[0]
    chunks = size // parts_of(size, max(1, size // 4))
    half = rows // 2
    return pl.pallas_call(
        functools.partial(gather_kernel, rows, chunks),
        out_shape=jax.ShapeDtypeStruct((rows * size,) + x.shape[1:], jnp.float32),
        in_specs=[pl.BlockSpec(memory_space=pltpu.VMEM)],
        out_specs=pl.BlockSpec(memory_space=pltpu.VMEM),
        scratch_shapes=[
            pltpu.SemaphoreType.DMA,
            pltpu.SemaphoreType.DMA((half, chunks)),
            pltpu.SemaphoreType.DMA((half, chunks)),
            pltpu.SemaphoreType.DMA((half, chunks)),
            pltpu.SemaphoreType.DMA((half, chunks)),
        ],
        compiler_params=pltpu.CompilerParams(
            collective_id=0, has_side_effects=True, vmem_limit_bytes=VMEM_BYTES
        ),
        name="gather",
    )(x)


def scatter_kernel(rows, chunks, g_ref, out_ref, pair, arrived, ssend_sem, srecv_sem, send_sem, recv_sem):
    half = rows // 2
    size = out_ref.shape[0]
    step = size // chunks
    r, c = lax.axis_index("row"), lax.axis_index("col")
    q, k = r // 2, r % 2
    sibling = r + 1 - 2 * k
    barrier = pltpu.get_barrier_semaphore()
    for d in range(1, half):
        pl.semaphore_signal(barrier, inc=1, device_id=((q + d) % half * 2 + k, c), device_id_type=MESH)
    pl.semaphore_signal(barrier, inc=1, device_id=(sibling, c), device_id_type=MESH)
    pl.semaphore_wait(barrier, half)

    def part(d, j, core):
        return pl.ds(((q + d) % half * 2 + core) * size + j * step, step)

    def to_sibling(d, j):
        return remote(g_ref.at[part(d, j, 1 - k)], pair.at[d, pl.ds(j * step, step)],
                      ssend_sem.at[d, j], srecv_sem.at[d, j], sibling, c)

    def send(d, j):
        return remote(pair.at[d, pl.ds(j * step, step)], arrived.at[d - 1, pl.ds(j * step, step)],
                      send_sem.at[d, j], recv_sem.at[d, j], (q + d) % half * 2 + k, c)

    order = list(range(1, half)) + [0]
    for j in range(chunks):
        for d in order:
            to_sibling(d, j).start()
    for j in range(chunks):
        here = pl.ds(j * step, step)
        for d in order:
            to_sibling(d, j).wait_recv()
            if d > 0:
                pair[d, here] = pair[d, here] + g_ref[part(d, j, k)]
                send(d, j).start()
            else:
                out_ref[here] = pair[0, here] + g_ref[part(0, j, k)]
    for j in range(chunks):
        here = pl.ds(j * step, step)
        total = out_ref[here]
        for d in range(1, half):
            send(d, j).wait_recv()
            total = total + arrived[d - 1, here]
        out_ref[here] = total
    for j in range(chunks):
        for d in range(half):
            to_sibling(d, j).wait_send()
            if d > 0:
                send(d, j).wait_send()


def scatter(g, rows):
    size = g.shape[0] // rows
    chunks = size // parts_of(size, max(1, size // 4))
    half = rows // 2
    tail = g.shape[1:]
    return pl.pallas_call(
        functools.partial(scatter_kernel, rows, chunks),
        out_shape=jax.ShapeDtypeStruct((size,) + tail, jnp.float32),
        in_specs=[pl.BlockSpec(memory_space=pltpu.VMEM)],
        out_specs=pl.BlockSpec(memory_space=pltpu.VMEM),
        scratch_shapes=[
            pltpu.VMEM((half, size) + tail, jnp.float32),
            pltpu.VMEM((half - 1, size) + tail, jnp.float32),
            pltpu.SemaphoreType.DMA((half, chunks)),
            pltpu.SemaphoreType.DMA((half, chunks)),
            pltpu.SemaphoreType.DMA((half, chunks)),
            pltpu.SemaphoreType.DMA((half, chunks)),
        ],
        compiler_params=pltpu.CompilerParams(
            collective_id=2, has_side_effects=True, vmem_limit_bytes=VMEM_BYTES
        ),
        name="scatter",
    )(g)


def chain_kernel(cols, ratio, chunks, x_ref, f_ref, row_ref, sum_ref, high, low, local_sem,
                 up_sem, down_sem, arrive_sem, rsend_sem, high_sem, low_sem):
    size = row_ref.shape[0]
    step = size // chunks
    r, c = lax.axis_index("row"), lax.axis_index("col")
    root = r // ratio
    base = r % ratio * size
    has_up, has_down = c < cols - 1, c > 0
    is_root, above, below = c == root, c > root, c < root
    barrier = pltpu.get_barrier_semaphore()

    @pl.when(has_up)
    def _():
        pl.semaphore_signal(barrier, inc=1, device_id=(r, c + 1), device_id_type=MESH)

    @pl.when(has_down)
    def _():
        pl.semaphore_signal(barrier, inc=1, device_id=(r, c - 1), device_id_type=MESH)

    pl.semaphore_wait(barrier, jnp.where(has_up, 1, 0) + jnp.where(has_down, 1, 0))

    def at(j):
        return pl.ds(j * step, step)

    def spread(source, sem, j, to):
        return remote(source, row_ref.at[at(j)], sem.at[j], arrive_sem.at[j], r, to)

    def spread_up(source, j):
        return spread(source, up_sem, j, c + 1)

    def spread_down(source, j):
        return spread(source, down_sem, j, c - 1)

    def sum_down(source, j):
        return remote(source.at[at(j)], high.at[at(j)], rsend_sem.at[j], high_sem.at[j], r, c - 1)

    def sum_up(source, j):
        return remote(source.at[at(j)], low.at[at(j)], rsend_sem.at[j], low_sem.at[j], r, c + 1)

    own = pltpu.make_async_copy(x_ref.at[pl.ds(base, size)], row_ref, local_sem)

    @pl.when(is_root)
    def _():
        for j in range(chunks):
            source = x_ref.at[pl.ds(base + j * step, step)]

            @pl.when(has_up)
            def _():
                spread_up(source, j).start()

            @pl.when(has_down)
            def _():
                spread_down(source, j).start()

        own.start()

    @pl.when(jnp.logical_and(above, c == cols - 1))
    def _():
        for j in range(chunks):
            sum_down(f_ref, j).start()

    @pl.when(jnp.logical_and(below, c == 0))
    def _():
        for j in range(chunks):
            sum_up(f_ref, j).start()

    for j in range(chunks):
        here = row_ref.at[at(j)]

        @pl.when(jnp.logical_not(is_root))
        def _():
            spread_up(here, j).wait_recv()

        @pl.when(jnp.logical_and(above, has_up))
        def _():
            spread_up(here, j).start()
            sum_down(f_ref, j).wait_recv()
            sum_ref[at(j)] = f_ref[at(j)] + high[at(j)]
            sum_down(sum_ref, j).start()

        @pl.when(jnp.logical_and(below, has_down))
        def _():
            spread_down(here, j).start()
            sum_up(f_ref, j).wait_recv()
            sum_ref[at(j)] = f_ref[at(j)] + low[at(j)]
            sum_up(sum_ref, j).start()

        @pl.when(is_root)
        def _():
            sum_ref[at(j)] = f_ref[at(j)]

            @pl.when(has_up)
            def _():
                sum_down(f_ref, j).wait_recv()
                sum_ref[at(j)] = sum_ref[at(j)] + high[at(j)]

            @pl.when(has_down)
            def _():
                sum_up(f_ref, j).wait_recv()
                sum_ref[at(j)] = sum_ref[at(j)] + low[at(j)]

    @pl.when(is_root)
    def _():
        own.wait()

    for j in range(chunks):
        here = row_ref.at[at(j)]

        @pl.when(jnp.logical_and(has_up, jnp.logical_or(is_root, above)))
        def _():
            spread_up(here, j).wait_send()

        @pl.when(jnp.logical_and(has_down, jnp.logical_or(is_root, below)))
        def _():
            spread_down(here, j).wait_send()

        @pl.when(jnp.logical_not(is_root))
        def _():
            sum_down(f_ref, j).wait_send()


def chain(x, f, cols, ratio):
    size = f.shape[0]
    chunks = size // parts_of(size, max(1, size // 8))
    whole = pl.BlockSpec(memory_space=pltpu.VMEM)
    shape = jax.ShapeDtypeStruct(f.shape, jnp.float32)
    sems = [pltpu.SemaphoreType.DMA((chunks,))] * 6
    return pl.pallas_call(
        functools.partial(chain_kernel, cols, ratio, chunks),
        out_shape=(shape, shape),
        in_specs=[whole, whole],
        out_specs=(whole, whole),
        scratch_shapes=[
            pltpu.VMEM(f.shape, jnp.float32),
            pltpu.VMEM(f.shape, jnp.float32),
            pltpu.SemaphoreType.DMA,
        ]
        + sems,
        compiler_params=pltpu.CompilerParams(
            collective_id=1, has_side_effects=True, vmem_limit_bytes=VMEM_BYTES
        ),
        name="chain",
    )(x, f)


def split(a):
    high = a.astype(jnp.bfloat16)
    return high, (a - high.astype(jnp.float32)).astype(jnp.bfloat16)


def product(x, a, contract):
    dims = (((1,), (contract,)), ((), ()))
    rows = x.shape[0]
    xh, xl = split(x)
    ah, al = split(a)
    both = lax.dot_general(jnp.concatenate([xh, xl], axis=0), ah, dims, preferred_element_type=jnp.float32)
    rest = lax.dot_general(xh, al, dims, preferred_element_type=jnp.float32)
    return both[:rows] + (both[rows:] + rest)


def products_kernel(group, contract, take_ref, put_ref, info_ref, x_ref, blocks_ref, *rest):
    out_ref = rest[-1]
    slots = blocks_ref.shape[0]
    first = pl.program_id(0) * slots
    count = info_ref[0]

    @pl.when(pl.program_id(0) == 0)
    def _():
        out_ref[...] = jnp.zeros_like(out_ref)
        if len(rest) == 2:
            add_ref = rest[0]

            @pl.when(info_ref[1] == 1)
            def _():
                out_ref[pl.ds(info_ref[2], add_ref.shape[0])] = add_ref[...]

    live = jnp.clip(count - first, 0, slots)

    def step(i, carry):
        at = i * group
        results = []
        for u in range(group):
            result = product(x_ref[take_ref[first + at + u]], blocks_ref[at + u], contract)
            results.append(jnp.where(at + u < live, result, 0.0))
        for u in range(group):
            place = put_ref[first + at + u]
            out_ref[place] = out_ref[place] + results[u]
        return carry

    lax.fori_loop(0, (live + group - 1) // group, step, 0)


def products(take, put, info, x, blocks, contract, out_blocks, add=None):
    total = blocks.shape[0]
    slots = parts_of(total, 44)
    group = parts_of(slots, 4)
    vecs = x.shape[1]
    whole = pl.BlockSpec(memory_space=pltpu.VMEM)
    in_specs = [whole, pl.BlockSpec((slots, BS, BS), lambda i, *_: (i, 0, 0))]
    operands = [x, blocks]
    if add is not None:
        in_specs.append(whole)
        operands.append(add)
    return pl.pallas_call(
        functools.partial(products_kernel, group, contract),
        out_shape=jax.ShapeDtypeStruct((out_blocks, vecs, BS), jnp.float32),
        grid_spec=pltpu.PrefetchScalarGridSpec(
            num_scalar_prefetch=3,
            grid=(total // slots,),
            in_specs=in_specs,
            out_specs=whole,
        ),
        compiler_params=pltpu.CompilerParams(vmem_limit_bytes=VMEM_BYTES),
        name="products",
    )(take, put, info, *operands)


def body(rows, cols, vectors, blocks, block_row, block_col, block_count, lower_bound, upper_bound):
    device_blocks = blocks[0, 0]
    rows_local, cols_local = block_row[0, 0], block_col[0, 0]
    ratio = rows // cols
    vecs, piece = vectors.shape
    col_blocks = piece * rows // BS
    row_blocks = piece * cols // BS
    row_index, col_index = lax.axis_index("row"), lax.axis_index("col")
    info = jnp.stack(
        [
            block_count[0, 0],
            (row_index // ratio == col_index).astype(jnp.int32),
            (row_index % ratio * row_blocks).astype(jnp.int32),
        ]
    )
    center = (upper_bound[0] + lower_bound[0]) / 2.0
    half_width = (upper_bound[0] - lower_bound[0]) / 2.0

    def apply_hamiltonian(x):
        col_tile = gather(x, rows)
        forward = products(cols_local, rows_local, info, col_tile, device_blocks, 1, row_blocks)
        row_tile, summed = chain(col_tile, forward, cols, ratio)
        backward = products(
            rows_local, cols_local, info, row_tile, device_blocks, 0, col_blocks, summed
        )
        return scatter(backward, rows)

    start = jnp.transpose(vectors.reshape(vecs, piece // BS, BS), (1, 0, 2))
    current = (apply_hamiltonian(start) - center * start) / half_width
    following = 2.0 * (apply_hamiltonian(current) - center * current) / half_width - start
    return jnp.transpose(following, (1, 0, 2)).reshape(vecs, piece)


def solution(mesh):
    placed = (
        P(None, ("col", "row")),
        P("row", "col", None, None, None),
        P("row", "col", None),
        P("row", "col", None),
        P("row", "col"),
        P(),
        P(),
    )
    return jax.shard_map(
        functools.partial(body, mesh.shape["row"], mesh.shape["col"]),
        mesh=mesh,
        in_specs=placed,
        out_specs=P(None, ("col", "row")),
        check_vma=False,
    )
```

```python
import functools

import jax
import jax.numpy as jnp
from jax import lax
from jax.experimental import pallas as pl
from jax.experimental.pallas import tpu as pltpu
from jax.sharding import PartitionSpec as P

BS = 128
VMEM_BYTES = 56 * 1024 * 1024
MESH = pl.DeviceIdType.MESH


def parts_of(total, most):
    best = 1
    for size in range(1, most + 1):
        if total % size == 0:
            best = size
    return best


def remote(src, dst, send_sem, recv_sem, row, col):
    return pltpu.make_async_remote_copy(
        src_ref=src,
        dst_ref=dst,
        send_sem=send_sem,
        recv_sem=recv_sem,
        device_id=(row, col),
        device_id_type=MESH,
    )


def gather_kernel(rows, chunks, x_ref, out_ref, local_sem, send_sem, recv_sem, fsend_sem, frecv_sem):
    half = rows // 2
    size = x_ref.shape[0]
    step = size // chunks
    r, c = lax.axis_index("row"), lax.axis_index("col")
    q, k = r // 2, r % 2
    sibling = r + 1 - 2 * k
    barrier = pltpu.get_barrier_semaphore()
    for d in range(1, half):
        pl.semaphore_signal(barrier, inc=1, device_id=((q + d) % half * 2 + k, c), device_id_type=MESH)
    pl.semaphore_signal(barrier, inc=1, device_id=(sibling, c), device_id_type=MESH)
    pl.semaphore_wait(barrier, half)

    def slot(owner, j):
        return out_ref.at[pl.ds(owner * size + j * step, step)]

    def send(d, j):
        return remote(x_ref.at[pl.ds(j * step, step)], slot(r, j), send_sem.at[d, j], recv_sem.at[d, j],
                      (q + d) % half * 2 + k, c)

    def pass_on(d, j):
        owner = (q + half - d) % half * 2 + k
        source = x_ref.at[pl.ds(j * step, step)] if d == 0 else slot(owner, j)
        return remote(source, slot(owner, j), fsend_sem.at[d, j], frecv_sem.at[d, j], sibling, c)

    for j in range(chunks):
        for d in range(1, half):
            send(d, j).start()
    for j in range(chunks):
        pass_on(0, j).start()
    own = pltpu.make_async_copy(x_ref, out_ref.at[pl.ds(r * size, size)], local_sem)
    own.start()
    for j in range(chunks):
        for d in range(1, half):
            send(d, j).wait_recv()
            pass_on(d, j).start()
    own.wait()
    for j in range(chunks):
        for d in range(half):
            pass_on(d, j).wait_recv()
            pass_on(d, j).wait_send()
            if d > 0:
                send(d, j).wait_send()


def gather(x, rows):
    size = x.shape[0]
    chunks = size // parts_of(size, max(1, size // 4))
    half = rows // 2
    return pl.pallas_call(
        functools.partial(gather_kernel, rows, chunks),
        out_shape=jax.ShapeDtypeStruct((rows * size,) + x.shape[1:], jnp.float32),
        in_specs=[pl.BlockSpec(memory_space=pltpu.VMEM)],
        out_specs=pl.BlockSpec(memory_space=pltpu.VMEM),
        scratch_shapes=[
            pltpu.SemaphoreType.DMA,
            pltpu.SemaphoreType.DMA((half, chunks)),
            pltpu.SemaphoreType.DMA((half, chunks)),
            pltpu.SemaphoreType.DMA((half, chunks)),
            pltpu.SemaphoreType.DMA((half, chunks)),
        ],
        compiler_params=pltpu.CompilerParams(
            collective_id=0, has_side_effects=True, vmem_limit_bytes=VMEM_BYTES
        ),
        name="gather",
    )(x)


def scatter_kernel(rows, chunks, g_ref, out_ref, pair, arrived, ssend_sem, srecv_sem, send_sem, recv_sem):
    half = rows // 2
    size = out_ref.shape[0]
    step = size // chunks
    r, c = lax.axis_index("row"), lax.axis_index("col")
    q, k = r // 2, r % 2
    sibling = r + 1 - 2 * k
    barrier = pltpu.get_barrier_semaphore()
    for d in range(1, half):
        pl.semaphore_signal(barrier, inc=1, device_id=((q + d) % half * 2 + k, c), device_id_type=MESH)
    pl.semaphore_signal(barrier, inc=1, device_id=(sibling, c), device_id_type=MESH)
    pl.semaphore_wait(barrier, half)

    def part(d, j, core):
        return pl.ds(((q + d) % half * 2 + core) * size + j * step, step)

    def to_sibling(d, j):
        return remote(g_ref.at[part(d, j, 1 - k)], pair.at[d, pl.ds(j * step, step)],
                      ssend_sem.at[d, j], srecv_sem.at[d, j], sibling, c)

    def send(d, j):
        return remote(pair.at[d, pl.ds(j * step, step)], arrived.at[d - 1, pl.ds(j * step, step)],
                      send_sem.at[d, j], recv_sem.at[d, j], (q + d) % half * 2 + k, c)

    order = list(range(1, half)) + [0]
    for j in range(chunks):
        for d in order:
            to_sibling(d, j).start()
    for j in range(chunks):
        here = pl.ds(j * step, step)
        for d in order:
            to_sibling(d, j).wait_recv()
            if d > 0:
                pair[d, here] = pair[d, here] + g_ref[part(d, j, k)]
                send(d, j).start()
            else:
                out_ref[here] = pair[0, here] + g_ref[part(0, j, k)]
    for j in range(chunks):
        here = pl.ds(j * step, step)
        total = out_ref[here]
        for d in range(1, half):
            send(d, j).wait_recv()
            total = total + arrived[d - 1, here]
        out_ref[here] = total
    for j in range(chunks):
        for d in range(half):
            to_sibling(d, j).wait_send()
            if d > 0:
                send(d, j).wait_send()


def scatter(g, rows):
    size = g.shape[0] // rows
    chunks = size // parts_of(size, max(1, size // 4))
    half = rows // 2
    tail = g.shape[1:]
    return pl.pallas_call(
        functools.partial(scatter_kernel, rows, chunks),
        out_shape=jax.ShapeDtypeStruct((size,) + tail, jnp.float32),
        in_specs=[pl.BlockSpec(memory_space=pltpu.VMEM)],
        out_specs=pl.BlockSpec(memory_space=pltpu.VMEM),
        scratch_shapes=[
            pltpu.VMEM((half, size) + tail, jnp.float32),
            pltpu.VMEM((half - 1, size) + tail, jnp.float32),
            pltpu.SemaphoreType.DMA((half, chunks)),
            pltpu.SemaphoreType.DMA((half, chunks)),
            pltpu.SemaphoreType.DMA((half, chunks)),
            pltpu.SemaphoreType.DMA((half, chunks)),
        ],
        compiler_params=pltpu.CompilerParams(
            collective_id=2, has_side_effects=True, vmem_limit_bytes=VMEM_BYTES
        ),
        name="scatter",
    )(g)


def chain_kernel(cols, ratio, chunks, x_ref, f_ref, row_ref, sum_ref, high, low, local_sem,
                 up_sem, down_sem, arrive_sem, rsend_sem, high_sem, low_sem):
    size = row_ref.shape[0]
    step = size // chunks
    r, c = lax.axis_index("row"), lax.axis_index("col")
    root = r // ratio
    base = r % ratio * size
    has_up, has_down = c < cols - 1, c > 0
    is_root, above, below = c == root, c > root, c < root
    barrier = pltpu.get_barrier_semaphore()

    @pl.when(has_up)
    def _():
        pl.semaphore_signal(barrier, inc=1, device_id=(r, c + 1), device_id_type=MESH)

    @pl.when(has_down)
    def _():
        pl.semaphore_signal(barrier, inc=1, device_id=(r, c - 1), device_id_type=MESH)

    pl.semaphore_wait(barrier, jnp.where(has_up, 1, 0) + jnp.where(has_down, 1, 0))

    def at(j):
        return pl.ds(j * step, step)

    def spread(source, sem, j, to):
        return remote(source, row_ref.at[at(j)], sem.at[j], arrive_sem.at[j], r, to)

    def spread_up(source, j):
        return spread(source, up_sem, j, c + 1)

    def spread_down(source, j):
        return spread(source, down_sem, j, c - 1)

    def sum_down(source, j):
        return remote(source.at[at(j)], high.at[at(j)], rsend_sem.at[j], high_sem.at[j], r, c - 1)

    def sum_up(source, j):
        return remote(source.at[at(j)], low.at[at(j)], rsend_sem.at[j], low_sem.at[j], r, c + 1)

    own = pltpu.make_async_copy(x_ref.at[pl.ds(base, size)], row_ref, local_sem)

    @pl.when(is_root)
    def _():
        for j in range(chunks):
            source = x_ref.at[pl.ds(base + j * step, step)]

            @pl.when(has_up)
            def _():
                spread_up(source, j).start()

            @pl.when(has_down)
            def _():
                spread_down(source, j).start()

        own.start()

    @pl.when(jnp.logical_and(above, c == cols - 1))
    def _():
        for j in range(chunks):
            sum_down(f_ref, j).start()

    @pl.when(jnp.logical_and(below, c == 0))
    def _():
        for j in range(chunks):
            sum_up(f_ref, j).start()

    lag = jnp.where(above, cols - 2 - c, c - 1) * 2

    def pass_on(t, carry):
        j = t - lag
        live = jnp.logical_and(j >= 0, j < chunks)

        @pl.when(t < chunks)
        def _():
            here = row_ref.at[at(t)]
            spread_up(here, t).wait_recv()

            @pl.when(jnp.logical_and(above, has_up))
            def _():
                spread_up(here, t).start()

            @pl.when(jnp.logical_and(below, has_down))
            def _():
                spread_down(here, t).start()

        @pl.when(jnp.logical_and(live, jnp.logical_and(above, has_up)))
        def _():
            sum_down(f_ref, j).wait_recv()
            sum_ref[at(j)] = f_ref[at(j)] + high[at(j)]
            sum_down(sum_ref, j).start()

        @pl.when(jnp.logical_and(live, jnp.logical_and(below, has_down)))
        def _():
            sum_up(f_ref, j).wait_recv()
            sum_ref[at(j)] = f_ref[at(j)] + low[at(j)]
            sum_up(sum_ref, j).start()

        return carry

    @pl.when(jnp.logical_not(is_root))
    def _():
        lax.fori_loop(0, chunks + 2 * max(cols - 3, 0), pass_on, 0)

    def take_in(j, carry):
        sum_ref[at(j)] = f_ref[at(j)]

        @pl.when(has_up)
        def _():
            sum_down(f_ref, j).wait_recv()
            sum_ref[at(j)] = sum_ref[at(j)] + high[at(j)]

        @pl.when(has_down)
        def _():
            sum_up(f_ref, j).wait_recv()
            sum_ref[at(j)] = sum_ref[at(j)] + low[at(j)]

        return carry

    @pl.when(is_root)
    def _():
        lax.fori_loop(0, chunks, take_in, 0)

    @pl.when(is_root)
    def _():
        own.wait()

    for j in range(chunks):
        here = row_ref.at[at(j)]

        @pl.when(jnp.logical_and(has_up, jnp.logical_or(is_root, above)))
        def _():
            spread_up(here, j).wait_send()

        @pl.when(jnp.logical_and(has_down, jnp.logical_or(is_root, below)))
        def _():
            spread_down(here, j).wait_send()

        @pl.when(jnp.logical_not(is_root))
        def _():
            sum_down(f_ref, j).wait_send()


def chain(x, f, cols, ratio):
    size = f.shape[0]
    chunks = size // parts_of(size, max(1, size // 16))
    whole = pl.BlockSpec(memory_space=pltpu.VMEM)
    shape = jax.ShapeDtypeStruct(f.shape, jnp.float32)
    sems = [pltpu.SemaphoreType.DMA((chunks,))] * 6
    return pl.pallas_call(
        functools.partial(chain_kernel, cols, ratio, chunks),
        out_shape=(shape, shape),
        in_specs=[whole, whole],
        out_specs=(whole, whole),
        scratch_shapes=[
            pltpu.VMEM(f.shape, jnp.float32),
            pltpu.VMEM(f.shape, jnp.float32),
            pltpu.SemaphoreType.DMA,
        ]
        + sems,
        compiler_params=pltpu.CompilerParams(
            collective_id=1, has_side_effects=True, vmem_limit_bytes=VMEM_BYTES
        ),
        name="chain",
    )(x, f)


def split(a):
    high = a.astype(jnp.bfloat16)
    return high, (a - high.astype(jnp.float32)).astype(jnp.bfloat16)


def product(x, a, contract):
    dims = (((1,), (contract,)), ((), ()))
    rows = x.shape[0]
    xh, xl = split(x)
    ah, al = split(a)
    both = lax.dot_general(jnp.concatenate([xh, xl], axis=0), ah, dims, preferred_element_type=jnp.float32)
    rest = lax.dot_general(xh, al, dims, preferred_element_type=jnp.float32)
    return both[:rows] + (both[rows:] + rest)


def products_kernel(group, contract, take_ref, put_ref, info_ref, x_ref, blocks_ref, *rest):
    out_ref = rest[-1]
    slots = blocks_ref.shape[0]
    first = pl.program_id(0) * slots
    count = info_ref[0]

    @pl.when(pl.program_id(0) == 0)
    def _():
        out_ref[...] = jnp.zeros_like(out_ref)
        if len(rest) == 2:
            add_ref = rest[0]

            @pl.when(info_ref[1] == 1)
            def _():
                out_ref[pl.ds(info_ref[2], add_ref.shape[0])] = add_ref[...]

    live = jnp.clip(count - first, 0, slots)

    def step(i, carry):
        at = i * group
        results = []
        for u in range(group):
            result = product(x_ref[take_ref[first + at + u]], blocks_ref[at + u], contract)
            results.append(jnp.where(at + u < live, result, 0.0))
        for u in range(group):
            place = put_ref[first + at + u]
            out_ref[place] = out_ref[place] + results[u]
        return carry

    lax.fori_loop(0, (live + group - 1) // group, step, 0)


def products(take, put, info, x, blocks, contract, out_blocks, add=None):
    total = blocks.shape[0]
    slots = parts_of(total, 44)
    group = parts_of(slots, 4)
    vecs = x.shape[1]
    whole = pl.BlockSpec(memory_space=pltpu.VMEM)
    in_specs = [whole, pl.BlockSpec((slots, BS, BS), lambda i, *_: (i, 0, 0))]
    operands = [x, blocks]
    if add is not None:
        in_specs.append(whole)
        operands.append(add)
    return pl.pallas_call(
        functools.partial(products_kernel, group, contract),
        out_shape=jax.ShapeDtypeStruct((out_blocks, vecs, BS), jnp.float32),
        grid_spec=pltpu.PrefetchScalarGridSpec(
            num_scalar_prefetch=3,
            grid=(total // slots,),
            in_specs=in_specs,
            out_specs=whole,
        ),
        compiler_params=pltpu.CompilerParams(vmem_limit_bytes=VMEM_BYTES),
        name="products",
    )(take, put, info, *operands)


def body(rows, cols, vectors, blocks, block_row, block_col, block_count, lower_bound, upper_bound):
    device_blocks = blocks[0, 0]
    rows_local, cols_local = block_row[0, 0], block_col[0, 0]
    ratio = rows // cols
    vecs, piece = vectors.shape
    col_blocks = piece * rows // BS
    row_blocks = piece * cols // BS
    row_index, col_index = lax.axis_index("row"), lax.axis_index("col")
    info = jnp.stack(
        [
            block_count[0, 0],
            (row_index // ratio == col_index).astype(jnp.int32),
            (row_index % ratio * row_blocks).astype(jnp.int32),
        ]
    )
    center = (upper_bound[0] + lower_bound[0]) / 2.0
    half_width = (upper_bound[0] - lower_bound[0]) / 2.0

    def apply_hamiltonian(x):
        col_tile = gather(x, rows)
        forward = products(cols_local, rows_local, info, col_tile, device_blocks, 1, row_blocks)
        row_tile, summed = chain(col_tile, forward, cols, ratio)
        backward = products(
            rows_local, cols_local, info, row_tile, device_blocks, 0, col_blocks, summed
        )
        return scatter(backward, rows)

    start = jnp.transpose(vectors.reshape(vecs, piece // BS, BS), (1, 0, 2))
    current = (apply_hamiltonian(start) - center * start) / half_width
    following = 2.0 * (apply_hamiltonian(current) - center * current) / half_width - start
    return jnp.transpose(following, (1, 0, 2)).reshape(vecs, piece)


def solution(mesh):
    placed = (
        P(None, ("col", "row")),
        P("row", "col", None, None, None),
        P("row", "col", None),
        P("row", "col", None),
        P("row", "col"),
        P(),
        P(),
    )
    return jax.shard_map(
        functools.partial(body, mesh.shape["row"], mesh.shape["col"]),
        mesh=mesh,
        in_specs=placed,
        out_specs=P(None, ("col", "row")),
        check_vma=False,
    )
```

```python
import functools

import jax
import jax.numpy as jnp
from jax import lax
from jax.experimental import pallas as pl
from jax.experimental.pallas import tpu as pltpu
from jax.sharding import PartitionSpec as P

BS = 128
VMEM_BYTES = 56 * 1024 * 1024
MESH = pl.DeviceIdType.MESH


def parts_of(total, most):
    best = 1
    for size in range(1, most + 1):
        if total % size == 0:
            best = size
    return best


def remote(src, dst, send_sem, recv_sem, row, col):
    return pltpu.make_async_remote_copy(
        src_ref=src,
        dst_ref=dst,
        send_sem=send_sem,
        recv_sem=recv_sem,
        device_id=(row, col),
        device_id_type=MESH,
    )


def gather_kernel(rows, chunks, x_ref, out_ref, local_sem, send_sem, recv_sem, fsend_sem, frecv_sem):
    half = rows // 2
    size = x_ref.shape[0]
    step = size // chunks
    r, c = lax.axis_index("row"), lax.axis_index("col")
    q, k = r // 2, r % 2
    sibling = r + 1 - 2 * k
    barrier = pltpu.get_barrier_semaphore()
    for d in range(1, half):
        pl.semaphore_signal(barrier, inc=1, device_id=((q + d) % half * 2 + k, c), device_id_type=MESH)
    pl.semaphore_signal(barrier, inc=1, device_id=(sibling, c), device_id_type=MESH)
    pl.semaphore_wait(barrier, half)

    def slot(owner, j):
        return out_ref.at[pl.ds(owner * size + j * step, step)]

    def send(d, j):
        return remote(x_ref.at[pl.ds(j * step, step)], slot(r, j), send_sem.at[d, j], recv_sem.at[d, j],
                      (q + d) % half * 2 + k, c)

    def pass_on(d, j):
        owner = (q + half - d) % half * 2 + k
        source = x_ref.at[pl.ds(j * step, step)] if d == 0 else slot(owner, j)
        return remote(source, slot(owner, j), fsend_sem.at[d, j], frecv_sem.at[d, j], sibling, c)

    for j in range(chunks):
        for d in range(1, half):
            send(d, j).start()
    for j in range(chunks):
        pass_on(0, j).start()
    own = pltpu.make_async_copy(x_ref, out_ref.at[pl.ds(r * size, size)], local_sem)
    own.start()
    for j in range(chunks):
        for d in range(1, half):
            send(d, j).wait_recv()
            pass_on(d, j).start()
    own.wait()
    for j in range(chunks):
        for d in range(half):
            pass_on(d, j).wait_recv()
            pass_on(d, j).wait_send()
            if d > 0:
                send(d, j).wait_send()


def gather(x, rows):
    size = x.shape[0]
    half = rows // 2
    chunks = size // parts_of(size, max(1, size // 8))
    kernel = functools.partial(gather_kernel, rows, chunks)
    if half == 4:
        kernel = functools.partial(square_gather_kernel, chunks)
    return pl.pallas_call(
        kernel,
        out_shape=jax.ShapeDtypeStruct((rows * size,) + x.shape[1:], jnp.float32),
        in_specs=[pl.BlockSpec(memory_space=pltpu.VMEM)],
        out_specs=pl.BlockSpec(memory_space=pltpu.VMEM),
        scratch_shapes=[
            pltpu.SemaphoreType.DMA,
            pltpu.SemaphoreType.DMA((half, chunks)),
            pltpu.SemaphoreType.DMA((half, chunks)),
            pltpu.SemaphoreType.DMA((half, chunks)),
            pltpu.SemaphoreType.DMA((half, chunks)),
        ],
        compiler_params=pltpu.CompilerParams(
            collective_id=0, has_side_effects=True, vmem_limit_bytes=VMEM_BYTES
        ),
        name="gather",
    )(x)


def scatter_kernel(rows, chunks, g_ref, out_ref, pair, arrived, ssend_sem, srecv_sem, send_sem, recv_sem):
    half = rows // 2
    size = out_ref.shape[0]
    step = size // chunks
    r, c = lax.axis_index("row"), lax.axis_index("col")
    q, k = r // 2, r % 2
    sibling = r + 1 - 2 * k
    barrier = pltpu.get_barrier_semaphore()
    for d in range(1, half):
        pl.semaphore_signal(barrier, inc=1, device_id=((q + d) % half * 2 + k, c), device_id_type=MESH)
    pl.semaphore_signal(barrier, inc=1, device_id=(sibling, c), device_id_type=MESH)
    pl.semaphore_wait(barrier, half)

    def part(d, j, core):
        return pl.ds(((q + d) % half * 2 + core) * size + j * step, step)

    def to_sibling(d, j):
        return remote(g_ref.at[part(d, j, 1 - k)], pair.at[d, pl.ds(j * step, step)],
                      ssend_sem.at[d, j], srecv_sem.at[d, j], sibling, c)

    def send(d, j):
        return remote(pair.at[d, pl.ds(j * step, step)], arrived.at[d - 1, pl.ds(j * step, step)],
                      send_sem.at[d, j], recv_sem.at[d, j], (q + d) % half * 2 + k, c)

    order = list(range(1, half)) + [0]
    for j in range(chunks):
        for d in order:
            to_sibling(d, j).start()
    for j in range(chunks):
        here = pl.ds(j * step, step)
        for d in order:
            to_sibling(d, j).wait_recv()
            if d > 0:
                pair[d, here] = pair[d, here] + g_ref[part(d, j, k)]
                send(d, j).start()
            else:
                out_ref[here] = pair[0, here] + g_ref[part(0, j, k)]
    for j in range(chunks):
        here = pl.ds(j * step, step)
        total = out_ref[here]
        for d in range(1, half):
            send(d, j).wait_recv()
            total = total + arrived[d - 1, here]
        out_ref[here] = total
    for j in range(chunks):
        for d in range(half):
            to_sibling(d, j).wait_send()
            if d > 0:
                send(d, j).wait_send()


def scatter(g, rows):
    size = g.shape[0] // rows
    half = rows // 2
    chunks = size // parts_of(size, max(1, size // 8))
    tail = g.shape[1:]
    kernel = functools.partial(scatter_kernel, rows, chunks)
    if half == 4:
        kernel = functools.partial(square_scatter_kernel, chunks)
    return pl.pallas_call(
        kernel,
        out_shape=jax.ShapeDtypeStruct((size,) + tail, jnp.float32),
        in_specs=[pl.BlockSpec(memory_space=pltpu.VMEM)],
        out_specs=pl.BlockSpec(memory_space=pltpu.VMEM),
        scratch_shapes=[
            pltpu.VMEM((half, size) + tail, jnp.float32),
            pltpu.VMEM((half - 1, size) + tail, jnp.float32),
            pltpu.SemaphoreType.DMA((half, chunks)),
            pltpu.SemaphoreType.DMA((half, chunks)),
            pltpu.SemaphoreType.DMA((half, chunks)),
            pltpu.SemaphoreType.DMA((half, chunks)),
        ],
        compiler_params=pltpu.CompilerParams(
            collective_id=2, has_side_effects=True, vmem_limit_bytes=VMEM_BYTES
        ),
        name="scatter",
    )(g)


def partners_of(q):
    return [q, q + 1 - q % 2 * 2, q + 2 - q // 2 * 4, 3 - q]


def greet_square(q, k, c, sibling):
    barrier = pltpu.get_barrier_semaphore()
    for d in (1, 2):
        pl.semaphore_signal(barrier, inc=1, device_id=(partners_of(q)[d] * 2 + k, c), device_id_type=MESH)
    pl.semaphore_signal(barrier, inc=1, device_id=(sibling, c), device_id_type=MESH)
    pl.semaphore_wait(barrier, 3)


def square_gather_kernel(chunks, x_ref, out_ref, local_sem, send_sem, recv_sem, fsend_sem, frecv_sem):
    size = x_ref.shape[0]
    step = size // chunks
    r, c = lax.axis_index("row"), lax.axis_index("col")
    q, k = r // 2, r % 2
    sibling = r + 1 - 2 * k
    partners = partners_of(q)
    greet_square(q, k, c, sibling)

    def slot(d, j):
        return out_ref.at[pl.ds((partners[d] * 2 + k) * size + j * step, step)]

    def mine(j):
        return x_ref.at[pl.ds(j * step, step)]

    def send(d, j):
        return remote(mine(j), slot(0, j), send_sem.at[d, j], recv_sem.at[d, j], partners[d] * 2 + k, c)

    def relay(j):
        first = 1 + j % 2
        source = slot(first, j)
        return remote(source, source, send_sem.at[3, j], recv_sem.at[3, j], partners[3 - first] * 2 + k, c)

    def pass_on(d, j):
        source = mine(j) if d == 0 else slot(d, j)
        return remote(source, slot(d, j), fsend_sem.at[d, j], frecv_sem.at[d, j], sibling, c)

    for j in range(chunks):
        for d in (1, 2):
            send(d, j).start()
    for j in range(chunks):
        pass_on(0, j).start()
    own = pltpu.make_async_copy(x_ref, out_ref.at[pl.ds(r * size, size)], local_sem)
    own.start()
    for t in range(chunks + 2):
        if t < chunks:
            for d in (1, 2):
                send(d, t).wait_recv()
                if d == 1 + t % 2:
                    relay(t).start()
                pass_on(d, t).start()
        if t >= 2:
            relay(t - 2).wait_recv()
            pass_on(3, t - 2).start()
    own.wait()
    for j in range(chunks):
        for d in range(4):
            pass_on(d, j).wait_recv()
            pass_on(d, j).wait_send()
        for d in (1, 2):
            send(d, j).wait_send()
        relay(j).wait_send()


def square_scatter_kernel(chunks, g_ref, out_ref, pair, arrived, ssend_sem, srecv_sem, send_sem, recv_sem):
    size = out_ref.shape[0]
    step = size // chunks
    r, c = lax.axis_index("row"), lax.axis_index("col")
    q, k = r // 2, r % 2
    sibling = r + 1 - 2 * k
    partners = partners_of(q)
    greet_square(q, k, c, sibling)

    def at(j):
        return pl.ds(j * step, step)

    def part(d, j, core):
        return pl.ds((partners[d] * 2 + core) * size + j * step, step)

    def to_sibling(d, j):
        return remote(g_ref.at[part(d, j, 1 - k)], pair.at[d, at(j)],
                      ssend_sem.at[d, j], srecv_sem.at[d, j], sibling, c)

    def send(d, j):
        to = 1 + j % 2 if d == 3 else d
        return remote(pair.at[d, at(j)], arrived.at[d - 1, at(j)],
                      send_sem.at[d, j], recv_sem.at[d, j], partners[to] * 2 + k, c)

    for j in range(chunks):
        for d in (3, 1 + j % 2, 2 - j % 2, 0):
            to_sibling(d, j).start()
    for t in range(chunks + 2):
        if t < chunks:
            for d in (3, 1 + t % 2, 2 - t % 2, 0):
                to_sibling(d, t).wait_recv()
                if d == 0:
                    out_ref[at(t)] = pair[0, at(t)] + g_ref[part(0, t, k)]
                else:
                    pair[d, at(t)] = pair[d, at(t)] + g_ref[part(d, t, k)]
                if d == 3 or d == 1 + t % 2:
                    send(d, t).start()
        if t >= 2:
            j = t - 2
            d = 2 - j % 2
            send(3, j).wait_recv()
            pair[d, at(j)] = pair[d, at(j)] + arrived[2, at(j)]
            send(d, j).start()
    for j in range(chunks):
        send(1, j).wait_recv()
        send(2, j).wait_recv()
        out_ref[at(j)] = out_ref[at(j)] + (arrived[0, at(j)] + arrived[1, at(j)])
    for j in range(chunks):
        for d in range(4):
            to_sibling(d, j).wait_send()
            if d > 0:
                send(d, j).wait_send()


def chain_kernel(cols, ratio, chunks, x_ref, f_ref, row_ref, sum_ref, high, low, local_sem,
                 up_sem, down_sem, arrive_sem, rsend_sem, high_sem, low_sem):
    size = row_ref.shape[0]
    step = size // chunks
    r, c = lax.axis_index("row"), lax.axis_index("col")
    root = r // ratio
    base = r % ratio * size
    has_up, has_down = c < cols - 1, c > 0
    is_root, above, below = c == root, c > root, c < root
    barrier = pltpu.get_barrier_semaphore()

    @pl.when(has_up)
    def _():
        pl.semaphore_signal(barrier, inc=1, device_id=(r, c + 1), device_id_type=MESH)

    @pl.when(has_down)
    def _():
        pl.semaphore_signal(barrier, inc=1, device_id=(r, c - 1), device_id_type=MESH)

    pl.semaphore_wait(barrier, jnp.where(has_up, 1, 0) + jnp.where(has_down, 1, 0))

    def at(j):
        return pl.ds(j * step, step)

    def spread(source, sem, j, to):
        return remote(source, row_ref.at[at(j)], sem.at[j], arrive_sem.at[j], r, to)

    def spread_up(source, j):
        return spread(source, up_sem, j, c + 1)

    def spread_down(source, j):
        return spread(source, down_sem, j, c - 1)

    def sum_down(source, j):
        return remote(source.at[at(j)], high.at[at(j)], rsend_sem.at[j], high_sem.at[j], r, c - 1)

    def sum_up(source, j):
        return remote(source.at[at(j)], low.at[at(j)], rsend_sem.at[j], low_sem.at[j], r, c + 1)

    own = pltpu.make_async_copy(x_ref.at[pl.ds(base, size)], row_ref, local_sem)

    @pl.when(is_root)
    def _():
        for j in range(chunks):
            source = x_ref.at[pl.ds(base + j * step, step)]

            @pl.when(has_up)
            def _():
                spread_up(source, j).start()

            @pl.when(has_down)
            def _():
                spread_down(source, j).start()

        own.start()

    @pl.when(jnp.logical_and(above, c == cols - 1))
    def _():
        for j in range(chunks):
            sum_down(f_ref, j).start()

    @pl.when(jnp.logical_and(below, c == 0))
    def _():
        for j in range(chunks):
            sum_up(f_ref, j).start()

    lag = jnp.where(above, cols - 2 - c, c - 1) * 2

    def pass_on(t, carry):
        j = t - lag
        live = jnp.logical_and(j >= 0, j < chunks)

        @pl.when(t < chunks)
        def _():
            here = row_ref.at[at(t)]
            spread_up(here, t).wait_recv()

            @pl.when(jnp.logical_and(above, has_up))
            def _():
                spread_up(here, t).start()

            @pl.when(jnp.logical_and(below, has_down))
            def _():
                spread_down(here, t).start()

        @pl.when(jnp.logical_and(live, jnp.logical_and(above, has_up)))
        def _():
            sum_down(f_ref, j).wait_recv()
            sum_ref[at(j)] = f_ref[at(j)] + high[at(j)]
            sum_down(sum_ref, j).start()

        @pl.when(jnp.logical_and(live, jnp.logical_and(below, has_down)))
        def _():
            sum_up(f_ref, j).wait_recv()
            sum_ref[at(j)] = f_ref[at(j)] + low[at(j)]
            sum_up(sum_ref, j).start()

        return carry

    @pl.when(jnp.logical_not(is_root))
    def _():
        lax.fori_loop(0, chunks + 2 * max(cols - 3, 0), pass_on, 0)

    def take_in(j, carry):
        sum_ref[at(j)] = f_ref[at(j)]

        @pl.when(has_up)
        def _():
            sum_down(f_ref, j).wait_recv()
            sum_ref[at(j)] = sum_ref[at(j)] + high[at(j)]

        @pl.when(has_down)
        def _():
            sum_up(f_ref, j).wait_recv()
            sum_ref[at(j)] = sum_ref[at(j)] + low[at(j)]

        return carry

    @pl.when(is_root)
    def _():
        lax.fori_loop(0, chunks, take_in, 0)

    @pl.when(is_root)
    def _():
        own.wait()

    for j in range(chunks):
        here = row_ref.at[at(j)]

        @pl.when(jnp.logical_and(has_up, jnp.logical_or(is_root, above)))
        def _():
            spread_up(here, j).wait_send()

        @pl.when(jnp.logical_and(has_down, jnp.logical_or(is_root, below)))
        def _():
            spread_down(here, j).wait_send()

        @pl.when(jnp.logical_not(is_root))
        def _():
            sum_down(f_ref, j).wait_send()


def chain(x, f, cols, ratio):
    size = f.shape[0]
    chunks = size // parts_of(size, max(1, size // 32))
    whole = pl.BlockSpec(memory_space=pltpu.VMEM)
    shape = jax.ShapeDtypeStruct(f.shape, jnp.float32)
    sems = [pltpu.SemaphoreType.DMA((chunks,))] * 6
    return pl.pallas_call(
        functools.partial(chain_kernel, cols, ratio, chunks),
        out_shape=(shape, shape),
        in_specs=[whole, whole],
        out_specs=(whole, whole),
        scratch_shapes=[
            pltpu.VMEM(f.shape, jnp.float32),
            pltpu.VMEM(f.shape, jnp.float32),
            pltpu.SemaphoreType.DMA,
        ]
        + sems,
        compiler_params=pltpu.CompilerParams(
            collective_id=1, has_side_effects=True, vmem_limit_bytes=VMEM_BYTES
        ),
        name="chain",
    )(x, f)


def split(a):
    high = a.astype(jnp.bfloat16)
    return high, (a - high.astype(jnp.float32)).astype(jnp.bfloat16)


def product(x, a, contract):
    dims = (((1,), (contract,)), ((), ()))
    rows = x.shape[0]
    xh, xl = split(x)
    ah, al = split(a)
    both = lax.dot_general(jnp.concatenate([xh, xl], axis=0), ah, dims, preferred_element_type=jnp.float32)
    rest = lax.dot_general(xh, al, dims, preferred_element_type=jnp.float32)
    return both[:rows] + (both[rows:] + rest)


def products_kernel(group, contract, take_ref, put_ref, info_ref, x_ref, blocks_ref, *rest):
    out_ref = rest[-1]
    slots = blocks_ref.shape[0]
    first = pl.program_id(0) * slots
    count = info_ref[0]

    @pl.when(pl.program_id(0) == 0)
    def _():
        out_ref[...] = jnp.zeros_like(out_ref)
        if len(rest) == 2:
            add_ref = rest[0]

            @pl.when(info_ref[1] == 1)
            def _():
                out_ref[pl.ds(info_ref[2], add_ref.shape[0])] = add_ref[...]

    live = jnp.clip(count - first, 0, slots)

    def step(i, carry):
        at = i * group
        results = []
        for u in range(group):
            result = product(x_ref[take_ref[first + at + u]], blocks_ref[at + u], contract)
            results.append(jnp.where(at + u < live, result, 0.0))
        for u in range(group):
            place = put_ref[first + at + u]
            out_ref[place] = out_ref[place] + results[u]
        return carry

    lax.fori_loop(0, (live + group - 1) // group, step, 0)


def products(take, put, info, x, blocks, contract, out_blocks, add=None):
    total = blocks.shape[0]
    slots = parts_of(total, 44)
    group = parts_of(slots, 4)
    vecs = x.shape[1]
    whole = pl.BlockSpec(memory_space=pltpu.VMEM)
    in_specs = [whole, pl.BlockSpec((slots, BS, BS), lambda i, *_: (i, 0, 0))]
    operands = [x, blocks]
    if add is not None:
        in_specs.append(whole)
        operands.append(add)
    return pl.pallas_call(
        functools.partial(products_kernel, group, contract),
        out_shape=jax.ShapeDtypeStruct((out_blocks, vecs, BS), jnp.float32),
        grid_spec=pltpu.PrefetchScalarGridSpec(
            num_scalar_prefetch=3,
            grid=(total // slots,),
            in_specs=in_specs,
            out_specs=whole,
        ),
        compiler_params=pltpu.CompilerParams(vmem_limit_bytes=VMEM_BYTES),
        name="products",
    )(take, put, info, *operands)


def body(rows, cols, vectors, blocks, block_row, block_col, block_count, lower_bound, upper_bound):
    device_blocks = blocks[0, 0]
    rows_local, cols_local = block_row[0, 0], block_col[0, 0]
    ratio = rows // cols
    vecs, piece = vectors.shape
    col_blocks = piece * rows // BS
    row_blocks = piece * cols // BS
    row_index, col_index = lax.axis_index("row"), lax.axis_index("col")
    info = jnp.stack(
        [
            block_count[0, 0],
            (row_index // ratio == col_index).astype(jnp.int32),
            (row_index % ratio * row_blocks).astype(jnp.int32),
        ]
    )
    center = (upper_bound[0] + lower_bound[0]) / 2.0
    half_width = (upper_bound[0] - lower_bound[0]) / 2.0

    def apply_hamiltonian(x):
        col_tile = gather(x, rows)
        forward = products(cols_local, rows_local, info, col_tile, device_blocks, 1, row_blocks)
        row_tile, summed = chain(col_tile, forward, cols, ratio)
        backward = products(
            rows_local, cols_local, info, row_tile, device_blocks, 0, col_blocks, summed
        )
        return scatter(backward, rows)

    start = jnp.transpose(vectors.reshape(vecs, piece // BS, BS), (1, 0, 2))
    current = (apply_hamiltonian(start) - center * start) / half_width
    following = 2.0 * (apply_hamiltonian(current) - center * current) / half_width - start
    return jnp.transpose(following, (1, 0, 2)).reshape(vecs, piece)


def solution(mesh):
    placed = (
        P(None, ("col", "row")),
        P("row", "col", None, None, None),
        P("row", "col", None),
        P("row", "col", None),
        P("row", "col"),
        P(),
        P(),
    )
    return jax.shard_map(
        functools.partial(body, mesh.shape["row"], mesh.shape["col"]),
        mesh=mesh,
        in_specs=placed,
        out_specs=P(None, ("col", "row")),
        check_vma=False,
    )
```

```python
import functools

import jax
import jax.numpy as jnp
from jax import lax
from jax.experimental import pallas as pl
from jax.experimental.pallas import tpu as pltpu
from jax.sharding import PartitionSpec as P

BS = 128
VMEM_BYTES = 56 * 1024 * 1024
MESH = pl.DeviceIdType.MESH
LAG = 4


def parts_of(total, most):
    best = 1
    for size in range(1, most + 1):
        if total % size == 0:
            best = size
    return best


def remote(src, dst, send_sem, recv_sem, row, col):
    return pltpu.make_async_remote_copy(
        src_ref=src,
        dst_ref=dst,
        send_sem=send_sem,
        recv_sem=recv_sem,
        device_id=(row, col),
        device_id_type=MESH,
    )


def gather_kernel(rows, chunks, x_ref, out_ref, local_sem, send_sem, recv_sem, fsend_sem, frecv_sem):
    half = rows // 2
    size = x_ref.shape[0]
    step = size // chunks
    r, c = lax.axis_index("row"), lax.axis_index("col")
    q, k = r // 2, r % 2
    sibling = r + 1 - 2 * k
    barrier = pltpu.get_barrier_semaphore()
    for d in range(1, half):
        pl.semaphore_signal(barrier, inc=1, device_id=((q + d) % half * 2 + k, c), device_id_type=MESH)
    pl.semaphore_signal(barrier, inc=1, device_id=(sibling, c), device_id_type=MESH)
    pl.semaphore_wait(barrier, half)

    def slot(owner, j):
        return out_ref.at[pl.ds(owner * size + j * step, step)]

    def send(d, j):
        return remote(x_ref.at[pl.ds(j * step, step)], slot(r, j), send_sem.at[d, j], recv_sem.at[d, j],
                      (q + d) % half * 2 + k, c)

    def pass_on(d, j):
        owner = (q + half - d) % half * 2 + k
        source = x_ref.at[pl.ds(j * step, step)] if d == 0 else slot(owner, j)
        return remote(source, slot(owner, j), fsend_sem.at[d, j], frecv_sem.at[d, j], sibling, c)

    for j in range(chunks):
        for d in range(1, half):
            send(d, j).start()
    for j in range(chunks):
        pass_on(0, j).start()
    own = pltpu.make_async_copy(x_ref, out_ref.at[pl.ds(r * size, size)], local_sem)
    own.start()
    for j in range(chunks):
        for d in range(1, half):
            send(d, j).wait_recv()
            pass_on(d, j).start()
    own.wait()
    for j in range(chunks):
        for d in range(half):
            pass_on(d, j).wait_recv()
            pass_on(d, j).wait_send()
            if d > 0:
                send(d, j).wait_send()


def gather(x, rows):
    size = x.shape[0]
    half = rows // 2
    chunks = size // parts_of(size, max(1, size // 8))
    kernel = functools.partial(gather_kernel, rows, chunks)
    if half == 4:
        kernel = functools.partial(square_gather_kernel, chunks)
    return pl.pallas_call(
        kernel,
        out_shape=jax.ShapeDtypeStruct((rows * size,) + x.shape[1:], jnp.float32),
        in_specs=[pl.BlockSpec(memory_space=pltpu.VMEM)],
        out_specs=pl.BlockSpec(memory_space=pltpu.VMEM),
        scratch_shapes=[
            pltpu.SemaphoreType.DMA,
            pltpu.SemaphoreType.DMA((half, chunks)),
            pltpu.SemaphoreType.DMA((half, chunks)),
            pltpu.SemaphoreType.DMA((half, chunks)),
            pltpu.SemaphoreType.DMA((half, chunks)),
        ],
        compiler_params=pltpu.CompilerParams(
            collective_id=0, has_side_effects=True, vmem_limit_bytes=VMEM_BYTES
        ),
        name="gather",
    )(x)


def scatter_kernel(rows, chunks, g_ref, out_ref, pair, arrived, ssend_sem, srecv_sem, send_sem, recv_sem):
    half = rows // 2
    size = out_ref.shape[0]
    step = size // chunks
    r, c = lax.axis_index("row"), lax.axis_index("col")
    q, k = r // 2, r % 2
    sibling = r + 1 - 2 * k
    barrier = pltpu.get_barrier_semaphore()
    for d in range(1, half):
        pl.semaphore_signal(barrier, inc=1, device_id=((q + d) % half * 2 + k, c), device_id_type=MESH)
    pl.semaphore_signal(barrier, inc=1, device_id=(sibling, c), device_id_type=MESH)
    pl.semaphore_wait(barrier, half)

    def part(d, j, core):
        return pl.ds(((q + d) % half * 2 + core) * size + j * step, step)

    def to_sibling(d, j):
        return remote(g_ref.at[part(d, j, 1 - k)], pair.at[d, pl.ds(j * step, step)],
                      ssend_sem.at[d, j], srecv_sem.at[d, j], sibling, c)

    def send(d, j):
        return remote(pair.at[d, pl.ds(j * step, step)], arrived.at[d - 1, pl.ds(j * step, step)],
                      send_sem.at[d, j], recv_sem.at[d, j], (q + d) % half * 2 + k, c)

    order = list(range(1, half)) + [0]
    for j in range(chunks):
        for d in order:
            to_sibling(d, j).start()
    for j in range(chunks):
        here = pl.ds(j * step, step)
        for d in order:
            to_sibling(d, j).wait_recv()
            if d > 0:
                pair[d, here] = pair[d, here] + g_ref[part(d, j, k)]
                send(d, j).start()
            else:
                out_ref[here] = pair[0, here] + g_ref[part(0, j, k)]
    for j in range(chunks):
        here = pl.ds(j * step, step)
        total = out_ref[here]
        for d in range(1, half):
            send(d, j).wait_recv()
            total = total + arrived[d - 1, here]
        out_ref[here] = total
    for j in range(chunks):
        for d in range(half):
            to_sibling(d, j).wait_send()
            if d > 0:
                send(d, j).wait_send()


def scatter(g, rows):
    size = g.shape[0] // rows
    half = rows // 2
    chunks = size // parts_of(size, max(1, size // 8))
    tail = g.shape[1:]
    kernel = functools.partial(scatter_kernel, rows, chunks)
    if half == 4:
        kernel = functools.partial(square_scatter_kernel, chunks)
    return pl.pallas_call(
        kernel,
        out_shape=jax.ShapeDtypeStruct((size,) + tail, jnp.float32),
        in_specs=[pl.BlockSpec(memory_space=pltpu.VMEM)],
        out_specs=pl.BlockSpec(memory_space=pltpu.VMEM),
        scratch_shapes=[
            pltpu.VMEM((half, size) + tail, jnp.float32),
            pltpu.VMEM((half - 1, size) + tail, jnp.float32),
            pltpu.SemaphoreType.DMA((half, chunks)),
            pltpu.SemaphoreType.DMA((half, chunks)),
            pltpu.SemaphoreType.DMA((half, chunks)),
            pltpu.SemaphoreType.DMA((half, chunks)),
        ],
        compiler_params=pltpu.CompilerParams(
            collective_id=2, has_side_effects=True, vmem_limit_bytes=VMEM_BYTES
        ),
        name="scatter",
    )(g)


def partners_of(q):
    return [q, q + 1 - q % 2 * 2, q + 2 - q // 2 * 4, 3 - q]


def greet_square(q, k, c, sibling):
    barrier = pltpu.get_barrier_semaphore()
    for d in (1, 2):
        pl.semaphore_signal(barrier, inc=1, device_id=(partners_of(q)[d] * 2 + k, c), device_id_type=MESH)
    pl.semaphore_signal(barrier, inc=1, device_id=(sibling, c), device_id_type=MESH)
    pl.semaphore_wait(barrier, 3)


def square_gather_kernel(chunks, x_ref, out_ref, local_sem, send_sem, recv_sem, fsend_sem, frecv_sem):
    size = x_ref.shape[0]
    step = size // chunks
    r, c = lax.axis_index("row"), lax.axis_index("col")
    q, k = r // 2, r % 2
    sibling = r + 1 - 2 * k
    partners = partners_of(q)
    greet_square(q, k, c, sibling)

    def slot(d, j):
        return out_ref.at[pl.ds((partners[d] * 2 + k) * size + j * step, step)]

    def mine(j):
        return x_ref.at[pl.ds(j * step, step)]

    def send(d, j):
        return remote(mine(j), slot(0, j), send_sem.at[d, j], recv_sem.at[d, j], partners[d] * 2 + k, c)

    def relay(j):
        first = 1 + j % 2
        source = slot(first, j)
        return remote(source, source, send_sem.at[3, j], recv_sem.at[3, j], partners[3 - first] * 2 + k, c)

    def pass_on(d, j):
        source = mine(j) if d == 0 else slot(d, j)
        return remote(source, slot(d, j), fsend_sem.at[d, j], frecv_sem.at[d, j], sibling, c)

    for j in range(chunks):
        for d in (1, 2):
            send(d, j).start()
    for j in range(chunks):
        pass_on(0, j).start()
    own = pltpu.make_async_copy(x_ref, out_ref.at[pl.ds(r * size, size)], local_sem)
    own.start()
    for t in range(chunks + 2):
        if t < chunks:
            for d in (1, 2):
                send(d, t).wait_recv()
                if d == 1 + t % 2:
                    relay(t).start()
                pass_on(d, t).start()
        if t >= 2:
            relay(t - 2).wait_recv()
            pass_on(3, t - 2).start()
    own.wait()
    for j in range(chunks):
        for d in range(4):
            pass_on(d, j).wait_recv()
            pass_on(d, j).wait_send()
        for d in (1, 2):
            send(d, j).wait_send()
        relay(j).wait_send()


def square_scatter_kernel(chunks, g_ref, out_ref, pair, arrived, ssend_sem, srecv_sem, send_sem, recv_sem):
    size = out_ref.shape[0]
    step = size // chunks
    r, c = lax.axis_index("row"), lax.axis_index("col")
    q, k = r // 2, r % 2
    sibling = r + 1 - 2 * k
    partners = partners_of(q)
    greet_square(q, k, c, sibling)

    def at(j):
        return pl.ds(j * step, step)

    def part(d, j, core):
        return pl.ds((partners[d] * 2 + core) * size + j * step, step)

    def to_sibling(d, j):
        return remote(g_ref.at[part(d, j, 1 - k)], pair.at[d, at(j)],
                      ssend_sem.at[d, j], srecv_sem.at[d, j], sibling, c)

    def send(d, j):
        to = 1 + j % 2 if d == 3 else d
        return remote(pair.at[d, at(j)], arrived.at[d - 1, at(j)],
                      send_sem.at[d, j], recv_sem.at[d, j], partners[to] * 2 + k, c)

    for j in range(chunks):
        for d in (3, 1 + j % 2, 2 - j % 2, 0):
            to_sibling(d, j).start()
    for t in range(chunks + 2):
        if t < chunks:
            for d in (3, 1 + t % 2, 2 - t % 2, 0):
                to_sibling(d, t).wait_recv()
                if d == 0:
                    out_ref[at(t)] = pair[0, at(t)] + g_ref[part(0, t, k)]
                else:
                    pair[d, at(t)] = pair[d, at(t)] + g_ref[part(d, t, k)]
                if d == 3 or d == 1 + t % 2:
                    send(d, t).start()
        if t >= 2:
            j = t - 2
            d = 2 - j % 2
            send(3, j).wait_recv()
            pair[d, at(j)] = pair[d, at(j)] + arrived[2, at(j)]
            send(d, j).start()
    for j in range(chunks):
        send(1, j).wait_recv()
        send(2, j).wait_recv()
        out_ref[at(j)] = out_ref[at(j)] + (arrived[0, at(j)] + arrived[1, at(j)])
    for j in range(chunks):
        for d in range(4):
            to_sibling(d, j).wait_send()
            if d > 0:
                send(d, j).wait_send()


def chain_kernel(cols, ratio, chunks, x_ref, f_ref, row_ref, sum_ref, high, low, local_sem,
                 up_sem, down_sem, arrive_sem, rsend_sem, high_sem, low_sem):
    size = row_ref.shape[0]
    step = size // chunks
    r, c = lax.axis_index("row"), lax.axis_index("col")
    root = r // ratio
    base = r % ratio * size
    has_up, has_down = c < cols - 1, c > 0
    is_root, above, below = c == root, c > root, c < root
    barrier = pltpu.get_barrier_semaphore()

    @pl.when(has_up)
    def _():
        pl.semaphore_signal(barrier, inc=1, device_id=(r, c + 1), device_id_type=MESH)

    @pl.when(has_down)
    def _():
        pl.semaphore_signal(barrier, inc=1, device_id=(r, c - 1), device_id_type=MESH)

    pl.semaphore_wait(barrier, jnp.where(has_up, 1, 0) + jnp.where(has_down, 1, 0))

    def at(j):
        return pl.ds(j * step, step)

    def spread(source, sem, j, to):
        return remote(source, row_ref.at[at(j)], sem.at[j], arrive_sem.at[j], r, to)

    def spread_up(source, j):
        return spread(source, up_sem, j, c + 1)

    def spread_down(source, j):
        return spread(source, down_sem, j, c - 1)

    def sum_down(source, j):
        return remote(source.at[at(j)], high.at[at(j)], rsend_sem.at[j], high_sem.at[j], r, c - 1)

    def sum_up(source, j):
        return remote(source.at[at(j)], low.at[at(j)], rsend_sem.at[j], low_sem.at[j], r, c + 1)

    own = pltpu.make_async_copy(x_ref.at[pl.ds(base, size)], row_ref, local_sem)

    @pl.when(is_root)
    def _():
        for j in range(chunks):
            source = x_ref.at[pl.ds(base + j * step, step)]

            @pl.when(has_up)
            def _():
                spread_up(source, j).start()

            @pl.when(has_down)
            def _():
                spread_down(source, j).start()

        own.start()

    @pl.when(jnp.logical_and(above, c == cols - 1))
    def _():
        for j in range(chunks):
            sum_down(f_ref, j).start()

    @pl.when(jnp.logical_and(below, c == 0))
    def _():
        for j in range(chunks):
            sum_up(f_ref, j).start()

    lag = jnp.where(above, cols - 2 - c, c - 1) * LAG

    def pass_on(t, carry):
        j = t - lag
        live = jnp.logical_and(j >= 0, j < chunks)

        @pl.when(t < chunks)
        def _():
            here = row_ref.at[at(t)]
            spread_up(here, t).wait_recv()

            @pl.when(jnp.logical_and(above, has_up))
            def _():
                spread_up(here, t).start()

            @pl.when(jnp.logical_and(below, has_down))
            def _():
                spread_down(here, t).start()

        @pl.when(jnp.logical_and(live, jnp.logical_and(above, has_up)))
        def _():
            sum_down(f_ref, j).wait_recv()
            sum_ref[at(j)] = f_ref[at(j)] + high[at(j)]
            sum_down(sum_ref, j).start()

        @pl.when(jnp.logical_and(live, jnp.logical_and(below, has_down)))
        def _():
            sum_up(f_ref, j).wait_recv()
            sum_ref[at(j)] = f_ref[at(j)] + low[at(j)]
            sum_up(sum_ref, j).start()

        return carry

    @pl.when(jnp.logical_not(is_root))
    def _():
        lax.fori_loop(0, chunks + LAG * max(cols - 3, 0), pass_on, 0)

    def take_in(j, carry):
        sum_ref[at(j)] = f_ref[at(j)]

        @pl.when(has_up)
        def _():
            sum_down(f_ref, j).wait_recv()
            sum_ref[at(j)] = sum_ref[at(j)] + high[at(j)]

        @pl.when(has_down)
        def _():
            sum_up(f_ref, j).wait_recv()
            sum_ref[at(j)] = sum_ref[at(j)] + low[at(j)]

        return carry

    @pl.when(is_root)
    def _():
        lax.fori_loop(0, chunks, take_in, 0)

    @pl.when(is_root)
    def _():
        own.wait()

    for j in range(chunks):
        here = row_ref.at[at(j)]

        @pl.when(jnp.logical_and(has_up, jnp.logical_or(is_root, above)))
        def _():
            spread_up(here, j).wait_send()

        @pl.when(jnp.logical_and(has_down, jnp.logical_or(is_root, below)))
        def _():
            spread_down(here, j).wait_send()

        @pl.when(jnp.logical_not(is_root))
        def _():
            sum_down(f_ref, j).wait_send()


def chain(x, f, cols, ratio):
    size = f.shape[0]
    chunks = size // parts_of(size, max(1, size // 32))
    whole = pl.BlockSpec(memory_space=pltpu.VMEM)
    shape = jax.ShapeDtypeStruct(f.shape, jnp.float32)
    sems = [pltpu.SemaphoreType.DMA((chunks,))] * 6
    return pl.pallas_call(
        functools.partial(chain_kernel, cols, ratio, chunks),
        out_shape=(shape, shape),
        in_specs=[whole, whole],
        out_specs=(whole, whole),
        scratch_shapes=[
            pltpu.VMEM(f.shape, jnp.float32),
            pltpu.VMEM(f.shape, jnp.float32),
            pltpu.SemaphoreType.DMA,
        ]
        + sems,
        compiler_params=pltpu.CompilerParams(
            collective_id=1, has_side_effects=True, vmem_limit_bytes=VMEM_BYTES
        ),
        name="chain",
    )(x, f)


def split(a):
    high = a.astype(jnp.bfloat16)
    return high, (a - high.astype(jnp.float32)).astype(jnp.bfloat16)


def product(x, a, contract):
    dims = (((1,), (contract,)), ((), ()))
    rows = x.shape[0]
    xh, xl = split(x)
    ah, al = split(a)
    both = lax.dot_general(jnp.concatenate([xh, xl], axis=0), ah, dims, preferred_element_type=jnp.float32)
    rest = lax.dot_general(xh, al, dims, preferred_element_type=jnp.float32)
    return both[:rows] + (both[rows:] + rest)


def products_kernel(group, contract, take_ref, put_ref, info_ref, x_ref, blocks_ref, *rest):
    out_ref = rest[-1]
    slots = blocks_ref.shape[0]
    first = pl.program_id(0) * slots
    count = info_ref[0]

    @pl.when(pl.program_id(0) == 0)
    def _():
        out_ref[...] = jnp.zeros_like(out_ref)
        if len(rest) == 2:
            add_ref = rest[0]

            @pl.when(info_ref[1] == 1)
            def _():
                out_ref[pl.ds(info_ref[2], add_ref.shape[0])] = add_ref[...]

    live = jnp.clip(count - first, 0, slots)

    def step(i, carry):
        at = i * group
        results = []
        for u in range(group):
            result = product(x_ref[take_ref[first + at + u]], blocks_ref[at + u], contract)
            results.append(jnp.where(at + u < live, result, 0.0))
        for u in range(group):
            place = put_ref[first + at + u]
            out_ref[place] = out_ref[place] + results[u]
        return carry

    lax.fori_loop(0, (live + group - 1) // group, step, 0)


def products(take, put, info, x, blocks, contract, out_blocks, add=None):
    total = blocks.shape[0]
    slots = parts_of(total, 44)
    group = parts_of(slots, 4)
    vecs = x.shape[1]
    whole = pl.BlockSpec(memory_space=pltpu.VMEM)
    in_specs = [whole, pl.BlockSpec((slots, BS, BS), lambda i, *_: (i, 0, 0))]
    operands = [x, blocks]
    if add is not None:
        in_specs.append(whole)
        operands.append(add)
    return pl.pallas_call(
        functools.partial(products_kernel, group, contract),
        out_shape=jax.ShapeDtypeStruct((out_blocks, vecs, BS), jnp.float32),
        grid_spec=pltpu.PrefetchScalarGridSpec(
            num_scalar_prefetch=3,
            grid=(total // slots,),
            in_specs=in_specs,
            out_specs=whole,
        ),
        compiler_params=pltpu.CompilerParams(vmem_limit_bytes=VMEM_BYTES),
        name="products",
    )(take, put, info, *operands)


def body(rows, cols, vectors, blocks, block_row, block_col, block_count, lower_bound, upper_bound):
    device_blocks = blocks[0, 0]
    rows_local, cols_local = block_row[0, 0], block_col[0, 0]
    ratio = rows // cols
    vecs, piece = vectors.shape
    col_blocks = piece * rows // BS
    row_blocks = piece * cols // BS
    row_index, col_index = lax.axis_index("row"), lax.axis_index("col")
    info = jnp.stack(
        [
            block_count[0, 0],
            (row_index // ratio == col_index).astype(jnp.int32),
            (row_index % ratio * row_blocks).astype(jnp.int32),
        ]
    )
    center = (upper_bound[0] + lower_bound[0]) / 2.0
    half_width = (upper_bound[0] - lower_bound[0]) / 2.0

    def apply_hamiltonian(x):
        col_tile = gather(x, rows)
        forward = products(cols_local, rows_local, info, col_tile, device_blocks, 1, row_blocks)
        row_tile, summed = chain(col_tile, forward, cols, ratio)
        backward = products(
            rows_local, cols_local, info, row_tile, device_blocks, 0, col_blocks, summed
        )
        return scatter(backward, rows)

    start = jnp.transpose(vectors.reshape(vecs, piece // BS, BS), (1, 0, 2))
    current = (apply_hamiltonian(start) - center * start) / half_width
    following = 2.0 * (apply_hamiltonian(current) - center * current) / half_width - start
    return jnp.transpose(following, (1, 0, 2)).reshape(vecs, piece)


def solution(mesh):
    placed = (
        P(None, ("col", "row")),
        P("row", "col", None, None, None),
        P("row", "col", None),
        P("row", "col", None),
        P("row", "col"),
        P(),
        P(),
    )
    return jax.shard_map(
        functools.partial(body, mesh.shape["row"], mesh.shape["col"]),
        mesh=mesh,
        in_specs=placed,
        out_specs=P(None, ("col", "row")),
        check_vma=False,
    )
```
